32 devices in a mesh: grp: 2 (over x), query: 16 (over z, y, core).
Axes of the slice: x: 2, y: 2, z: 4, core: 2. Of those that a mesh axis runs over, the one named last changes fastest.
Arguments:
- acts: bfloat16 [8192, 8192], P(('grp', 'query')), parts along dimension 0, may hold values from -6 to 6
- grads: bfloat16 [8192, 14336], P(('grp', 'query')), parts along dimension 0, may hold values from -6 to 6
- u_factor: bfloat16 [28672, 512], P(('grp', 'query')), parts along dimension 0, may hold values from -0.00018310547 to 0.00018310547
- v_factor: bfloat16 [16384, 512], P(('grp', 'query')), parts along dimension 0, may hold values from -0.0625 to 0.0625
- lengths: int32 [4], P('grp'), parts along dimension 0, may hold values from 1 to 2048, 3072 in all
Outputs:
- scores: float32 [32, 2], P('grp'), parts along dimension 0
The draws below stay inside these ranges and needn't reach their ends.
There are 2 independent parts, one for each index of `grp`. The reference program is written for one: setup_inputs(seed, part) draws one part's arguments, and reference() takes and returns one part's arrays. A program takes and returns all parts, laid end to end along the dimension named above; each array names one. Nothing has to cross between parts.
Inputs may be any that keep to these rules, and one draw needn't show every extreme that they name: Sequence s owns token slots s * 2048 to (s + 1) * 2048 - 1, of which the first lengths[s] are live; the counts sum to three quarters of 4096.
All inputs are finite; a program needn't handle non-finite values.
Results may differ from the reference program's by a relative error of at most 0.0003.
Values may be sent and summed in bfloat16 or wider, within the bound.
A program may use at most 128 MiB of HBM per device.

```python
import math
import jax
import jax.numpy as jnp
import numpy as np

DIN = 8192
FFW = 14336
RANK = 32
QUERIES = 16
LENGTH = 2048
TOKENS = 4096
SEQS = 2


def steps_of(own_key, dims, pieces, low, top_value):
    def one(axis_at, blocks):
        steps = jax.random.uniform(jax.random.fold_in(jax.random.fold_in(own_key, 6), axis_at), (blocks,), jnp.float32, low / len(pieces), top_value / len(pieces))
        return jnp.repeat(jnp.exp(steps), dims[axis_at] // blocks).reshape((-1,) + (1,) * (len(dims) - axis_at - 1))

    factor_of = one(*pieces[0])
    for cut in pieces[1:]:
        factor_of = factor_of * one(*cut)
    return factor_of


def profile(number_of, total, bound, skew):
    loads = [(1 << 20) // math.isqrt(rank ** skew) + 1 for rank in range(2, number_of + 1)]
    rest, counts = total - bound - (number_of - 1), [1] * (number_of - 1)
    while rest > 0:
        candidates = [i for i in range(number_of - 1) if counts[i] < bound]
        mass, remaining = sum([loads[i] for i in candidates]), rest
        for i in candidates:
            extra = min(bound - counts[i], max(1, remaining * loads[i] // mass), rest)
            counts[i] = counts[i] + extra
            rest = rest - extra
    return np.array([bound] + counts)


def uneven_parts(rng, number_of, total, reach, lean):
    if number_of == 2:
        one = jax.random.randint(rng, (), max(1, total - reach), min(reach, total - 1) + 1)
        return jnp.stack([one, total - one])
    sizes = jnp.asarray(profile(number_of, total, reach, lean), jnp.int32)
    couples = (number_of - 1) // 2
    giver, taker = sizes[1:1 + 2 * couples:2], sizes[2:2 + 2 * couples:2]
    slack = jnp.minimum(giver - 1, reach - taker)
    moved = jax.random.randint(jax.random.fold_in(rng, 1), (couples,), 0, 1 << 20) % (slack + 1)
    sizes = sizes.at[1:1 + 2 * couples:2].set(giver - moved).at[2:2 + 2 * couples:2].set(taker + moved)
    return sizes[jax.random.permutation(jax.random.fold_in(rng, 2), number_of)]


def gaussian(stream_key, dims, spread, limit, pieces=(), kind=jnp.bfloat16):
    result = jax.random.normal(stream_key, dims, jnp.float32) * spread
    if len(pieces) > 0:
        result = steps_of(stream_key, dims, pieces, -0.22, 0.18) * result
    return jnp.clip(result, min=-limit, max=limit).astype(kind)


def setup_inputs(seed: int = 0, part: int = 0) -> dict:
    key_list = jax.random.split(jax.random.key(seed), 6)
    part_splits = jax.random.split(jax.random.fold_in(key_list[5], part), 6)
    acts = gaussian(part_splits[0], (TOKENS, DIN), 1.0, 6.0, ((0, 16),))
    grads = gaussian(part_splits[1], (TOKENS, FFW), 1.0, 6.0, ((0, 16),))
    u_factor = gaussian(part_splits[2], (FFW, QUERIES * RANK), (FFW * RANK * LENGTH) ** -0.5, 0.00018310547, ((0, 16),))
    v_factor = gaussian(part_splits[3], (DIN, QUERIES * RANK), DIN ** -0.5, 0.0625, ((0, 16),))
    lengths = uneven_parts(part_splits[4], SEQS, 3 * SEQS * LENGTH // 4, LENGTH, 2).astype(jnp.int32)
    return dict(acts=acts, grads=grads, u_factor=u_factor, v_factor=v_factor, lengths=lengths)


def reference(acts, grads, u_factor, v_factor, lengths):
    out_proj = jnp.dot(grads, u_factor, preferred_element_type=jnp.float32)
    in_proj = jnp.dot(acts, v_factor, preferred_element_type=jnp.float32)
    token_score = (out_proj * in_proj).reshape(TOKENS, QUERIES, RANK).sum(axis=2)
    slots = jnp.arange(TOKENS, dtype=jnp.int32)
    seq_index = slots // LENGTH
    position = slots % LENGTH
    live = position < lengths[seq_index]
    token_score = jnp.where(live[:, None], token_score, jnp.zeros_like(token_score))
    per_seq = token_score.reshape(SEQS, LENGTH, QUERIES).sum(axis=1)
    return per_seq.T
```

```python
import functools

import jax
import jax.numpy as jnp
from jax import lax
from jax.experimental import pallas as pl
from jax.experimental.pallas import tpu as pltpu
from jax.sharding import PartitionSpec as P

RANK = 32
LENGTH = 2048
MESH = pl.DeviceIdType.MESH
DEPTH, WIDTH, CORES = 4, 2, 2
UP, DOWN, ACROSS, SIBLING = range(4)


def device(z, y, core):
    return (z * WIDTH + y) * CORES + core


def nearest(z, rank):
    near = jnp.where(z < 2, z, 3 - z)
    swapped = jnp.where(rank == 0, 1, jnp.where(rank == 1, 0, rank))
    found = jnp.where(near == 0, rank, swapped)
    return jnp.where(z < 2, found, 3 - found)


def kernel(pieces, lengths, grads, acts, u_own, v_own, out, u_all, v_all, grads_here, acts_here, out_proj, in_proj,
           parts, load_sem, send_sem, recv_sem, part_send_sem, part_recv_sem):
    me = lax.axis_index("query")
    members = u_all.shape[0]
    core = lax.rem(me, CORES)
    y = lax.rem(me // CORES, WIDTH)
    z = me // (CORES * WIDTH)
    sibling = device(z, y, 1 - core)
    across = device(z, 1 - y, core)
    u_rows, v_rows = u_own.shape[0], v_own.shape[0]
    rows = grads.shape[0]

    loads = [
        pltpu.make_async_copy(u_own, u_all.at[me], load_sem.at[0]),
        pltpu.make_async_copy(v_own, v_all.at[me], load_sem.at[1]),
        pltpu.make_async_copy(grads, grads_here, load_sem.at[2]),
        pltpu.make_async_copy(acts, acts_here, load_sem.at[3]),
    ]
    for load in loads:
        load.start()

    barrier = pltpu.get_barrier_semaphore()

    @pl.loop(1, members)
    def _(step):
        pl.semaphore_signal(barrier, inc=1, device_id={"query": lax.rem(me + step, members)}, device_id_type=MESH)

    pl.semaphore_wait(barrier, members - 1)

    def piece(owner, kind):
        side, start, size = pieces[kind]
        return (u_all if side == 0 else v_all).at[owner, pl.ds(start, size)]

    def copy(owner, kind, way, target):
        return pltpu.make_async_remote_copy(
            src_ref=piece(owner, kind),
            dst_ref=piece(owner, kind),
            send_sem=send_sem.at[way, owner, kind],
            recv_sem=recv_sem.at[owner, kind],
            device_id={"query": target},
            device_id_type=MESH,
        )

    def start(one):
        one.start()

    def drain(one):
        one.wait_send()

    def arrived(owner, kind):
        copy(owner, kind, SIBLING, sibling).wait_recv()

    last = len(pieces) - 1
    direct = tuple(range(last))

    def along(act, owner, kind, up, down):
        @pl.when(up)
        def _():
            act(copy(owner, kind, UP, device(z + 1, y, core)))

        @pl.when(down)
        def _():
            act(copy(owner, kind, DOWN, device(z - 1, y, core)))

    def over(act, owner, kind):
        act(copy(owner, kind, ACROSS, across))

    def beside(act, owner, kind):
        act(copy(owner, kind, SIBLING, sibling))

    def send_own(act):
        up, down = z < DEPTH - 1, z > 0
        over(act, me, last)
        along(act, me, last, up, down)
        for kind in direct:
            along(act, me, kind, up, down)
            over(act, me, kind)
        for kind in range(last + 1):
            beside(act, me, kind)

    def send_neighbours(act, wait):
        wait(across, last)
        along(act, across, last, z < DEPTH - 1, z > 0)
        beside(act, across, last)

    def send_line(act, wait, rank):
        other = nearest(z, rank)
        up = jnp.logical_and(other < z, z < DEPTH - 1)
        down = jnp.logical_and(other > z, z > 0)
        same, opposite = device(other, y, core), device(other, 1 - y, core)
        wait(same, last)
        along(act, same, last, up, down)
        beside(act, same, last)
        for kind in direct:
            wait(same, kind)
            along(act, same, kind, up, down)
            over(act, same, kind)
            beside(act, same, kind)
        wait(opposite, last)
        along(act, opposite, last, up, down)
        beside(act, opposite, last)

    def send_crossed(act, wait, rank):
        opposite = device(nearest(z, rank), 1 - y, core)
        for kind in direct:
            wait(opposite, kind)
            beside(act, opposite, kind)

    def multiply(owner):
        u_columns = pl.ds(pl.multiple_of(owner * u_rows, 128), u_rows)
        v_columns = pl.ds(pl.multiple_of(owner * v_rows, 128), v_rows)
        out_proj[...] += jnp.dot(grads_here[:, u_columns], u_all[owner], preferred_element_type=jnp.float32)
        in_proj[...] += jnp.dot(acts_here[:, v_columns], v_all[owner], preferred_element_type=jnp.float32)

    def multiply_chip(other_z, other_y):
        @pl.loop(0, CORES)
        def _(turn):
            owner = device(other_z, other_y, jnp.where(turn == 0, core, 1 - core))

            @pl.when(turn == 1)
            def _():
                for kind in range(last + 1):
                    arrived(owner, kind)

            multiply(owner)

    loads[0].wait()
    loads[1].wait()
    send_own(start)
    out_proj[...] = jnp.zeros_like(out_proj)
    in_proj[...] = jnp.zeros_like(in_proj)
    send_neighbours(start, arrived)
    loads[2].wait()
    loads[3].wait()
    multiply_chip(z, y)

    @pl.loop(1, DEPTH)
    def _(rank):
        send_line(start, arrived, rank)
        send_crossed(start, arrived, rank - 1)
        multiply_chip(nearest(z, rank - 1), 1 - y)
        multiply_chip(nearest(z, rank), y)

    send_crossed(start, arrived, DEPTH - 1)
    multiply_chip(nearest(z, DEPTH - 1), 1 - y)

    first_slot = me * rows
    live_count = lengths[first_slot // LENGTH]
    offsets = lax.rem(first_slot, LENGTH) + lax.broadcasted_iota(jnp.int32, out_proj.shape, 0)
    product = out_proj[...] * in_proj[...]
    parts[me] = jnp.sum(jnp.where(offsets < live_count, product, 0.0), axis=0, keepdims=True)

    def part_copy(step):
        target = lax.rem(me + step, members)
        return pltpu.make_async_remote_copy(
            src_ref=parts.at[me],
            dst_ref=parts.at[me],
            send_sem=part_send_sem.at[step],
            recv_sem=part_recv_sem.at[step],
            device_id={"query": target},
            device_id_type=MESH,
        )

    @pl.loop(1, members)
    def _(step):
        part_copy(step).start()

    def no_wait(owner, kind):
        pass

    send_own(drain)
    send_neighbours(drain, no_wait)

    @pl.loop(1, DEPTH)
    def _(rank):
        send_line(drain, no_wait, rank)

    @pl.loop(0, DEPTH)
    def _(rank):
        send_crossed(drain, no_wait, rank)

    @pl.loop(1, members)
    def _(step):
        part_copy(step).wait()

    query_count, seq_count = out.shape
    shape = (query_count, parts.shape[2])
    mine = lax.broadcasted_iota(jnp.int32, shape, 1) // RANK == lax.broadcasted_iota(jnp.int32, shape, 0)
    columns = []
    for seq in range(seq_count):
        total = sum(parts[owner] for owner in range(members) if owner * rows // LENGTH == seq)
        columns.append(jnp.sum(jnp.where(mine, total, 0.0), axis=1, keepdims=True))
    out[...] = jnp.concatenate(columns, axis=1)


def fused(acts, grads, u_factor, v_factor, lengths):
    members = lax.axis_size("query")
    rows, factor_cols = acts.shape[0], u_factor.shape[1]
    u_rows, v_rows = u_factor.shape[0], v_factor.shape[0]
    u_cut = -(-u_rows // 256) * 128
    v_cut = v_rows // 256 * 128
    pieces = ((0, 0, u_cut), (0, u_cut, u_rows - u_cut), (1, 0, v_cut), (1, v_cut, v_rows - v_cut))
    hbm = pl.BlockSpec(memory_space=pl.ANY)
    return pl.pallas_call(
        functools.partial(kernel, pieces),
        out_shape=jax.ShapeDtypeStruct((factor_cols // RANK, lengths.shape[0]), jnp.float32),
        in_specs=[pl.BlockSpec(memory_space=pltpu.SMEM), hbm, hbm, hbm, hbm],
        out_specs=pl.BlockSpec(memory_space=pltpu.VMEM),
        scratch_shapes=[
            pltpu.VMEM((members, u_rows, factor_cols), u_factor.dtype),
            pltpu.VMEM((members, v_rows, factor_cols), v_factor.dtype),
            pltpu.VMEM(grads.shape, grads.dtype),
            pltpu.VMEM(acts.shape, acts.dtype),
            pltpu.VMEM((rows, factor_cols), jnp.float32),
            pltpu.VMEM((rows, factor_cols), jnp.float32),
            pltpu.VMEM((members, 1, factor_cols), jnp.float32),
            pltpu.SemaphoreType.DMA((4,)),
            pltpu.SemaphoreType.DMA((4, members, len(pieces))),
            pltpu.SemaphoreType.DMA((members, len(pieces))),
            pltpu.SemaphoreType.DMA((members,)),
            pltpu.SemaphoreType.DMA((members,)),
        ],
        compiler_params=pltpu.CompilerParams(
            collective_id=0, has_side_effects=True, vmem_limit_bytes=56 * 1024 * 1024
        ),
        cost_estimate=pl.CostEstimate(
            flops=2 * rows * factor_cols * members * (u_rows + v_rows),
            bytes_accessed=2 * (acts.size + grads.size + u_factor.size + v_factor.size),
            transcendentals=0,
        ),
    )(lengths, grads, acts, u_factor, v_factor)


def gathered(acts, grads, u_factor, v_factor, lengths):
    rows_here = acts.shape[0]
    members = lax.axis_size("query")
    factor_cols = u_factor.shape[1]
    grads_blocks = grads.reshape(rows_here, members, u_factor.shape[0])
    acts_blocks = acts.reshape(rows_here, members, v_factor.shape[0])
    u_whole = lax.all_gather(u_factor[None], "query", axis=0, tiled=True)
    v_whole = lax.all_gather(v_factor[None], "query", axis=0, tiled=True)
    out_proj = jnp.einsum("tkf,kfc->tc", grads_blocks, u_whole, preferred_element_type=jnp.float32)
    in_proj = jnp.einsum("tkf,kfc->tc", acts_blocks, v_whole, preferred_element_type=jnp.float32)
    token_score = (out_proj * in_proj).reshape(rows_here, factor_cols // RANK, RANK).sum(axis=2)
    first_slot = lax.axis_index("query") * rows_here
    offsets = first_slot % LENGTH + jnp.arange(rows_here, dtype=jnp.int32)
    selector = jnp.arange(lengths.shape[0], dtype=jnp.int32) == first_slot // LENGTH
    live_count = jnp.sum(jnp.where(selector, lengths, jnp.zeros_like(lengths)))
    live = (offsets < live_count).astype(jnp.float32)
    query_sums = jnp.sum(token_score * live[:, None], axis=0)
    return lax.psum(query_sums[:, None] * selector.astype(jnp.float32)[None, :], "query")


def solution(mesh):
    whole_grid = mesh.shape["query"] == DEPTH * WIDTH * CORES
    return jax.shard_map(
        fused if whole_grid else gathered,
        mesh=mesh,
        in_specs=(
            P(("grp", "query"), None),
            P(("grp", "query"), None),
            P(("grp", "query"), None),
            P(("grp", "query"), None),
            P("grp"),
        ),
        out_specs=P("grp", None),
        check_vma=False,
    )
```

```python
import functools

import jax
import jax.numpy as jnp
from jax import lax
from jax.experimental import pallas as pl
from jax.experimental.pallas import tpu as pltpu
from jax.sharding import PartitionSpec as P

RANK = 32
LENGTH = 2048
MESH = pl.DeviceIdType.MESH
DEPTH, WIDTH, CORES = 4, 2, 2
UP, DOWN, ACROSS, SIBLING = range(4)


def device(z, y, core):
    return (z * WIDTH + y) * CORES + core


def nearest(z, rank):
    near = jnp.where(z < 2, z, 3 - z)
    swapped = jnp.where(rank == 0, 1, jnp.where(rank == 1, 0, rank))
    found = jnp.where(near == 0, rank, swapped)
    return jnp.where(z < 2, found, 3 - found)


def kernel(pieces, lengths, grads, acts, u_own, v_own, out, u_all, v_all, grads_here, acts_here, out_proj, in_proj,
           parts, load_sem, send_sem, recv_sem, part_send_sem, part_recv_sem):
    me = lax.axis_index("query")
    members = u_all.shape[0]
    core = lax.rem(me, CORES)
    y = lax.rem(me // CORES, WIDTH)
    z = me // (CORES * WIDTH)
    sibling = device(z, y, 1 - core)
    across = device(z, 1 - y, core)
    u_rows, v_rows = u_own.shape[0], v_own.shape[0]
    rows = grads.shape[0]

    loads = [
        pltpu.make_async_copy(u_own, u_all.at[me], load_sem.at[0]),
        pltpu.make_async_copy(v_own, v_all.at[me], load_sem.at[1]),
        pltpu.make_async_copy(grads, grads_here, load_sem.at[2]),
        pltpu.make_async_copy(acts, acts_here, load_sem.at[3]),
    ]
    for load in loads:
        load.start()

    barrier = pltpu.get_barrier_semaphore()

    @pl.loop(1, members)
    def _(step):
        pl.semaphore_signal(barrier, inc=1, device_id={"query": lax.rem(me + step, members)}, device_id_type=MESH)

    pl.semaphore_wait(barrier, members - 1)

    def piece(owner, kind):
        side, start, size = pieces[kind]
        return (u_all if side == 0 else v_all).at[owner, pl.ds(start, size)]

    def copy(owner, kind, way, target):
        return pltpu.make_async_remote_copy(
            src_ref=piece(owner, kind),
            dst_ref=piece(owner, kind),
            send_sem=send_sem.at[way, owner, kind],
            recv_sem=recv_sem.at[owner, kind],
            device_id={"query": target},
            device_id_type=MESH,
        )

    def start(one):
        one.start()

    def drain(one):
        one.wait_send()

    def arrived(owner, kind):
        copy(owner, kind, SIBLING, sibling).wait_recv()

    last = len(pieces) - 1
    direct = tuple(range(last))

    def along(act, owner, kind, up, down):
        @pl.when(up)
        def _():
            act(copy(owner, kind, UP, device(z + 1, y, core)))

        @pl.when(down)
        def _():
            act(copy(owner, kind, DOWN, device(z - 1, y, core)))

    def over(act, owner, kind):
        act(copy(owner, kind, ACROSS, across))

    def beside(act, owner, kind):
        act(copy(owner, kind, SIBLING, sibling))

    corner = jnp.logical_or(z == 0, z == DEPTH - 1)
    inner = jnp.logical_not(corner)

    def send_own(act):
        over(act, me, last)
        for kind in direct:
            along(act, me, kind, z < DEPTH - 1, z > 0)
            over(act, me, kind)
        for kind in range(last + 1):
            beside(act, me, kind)

    def send_home_turned(act, up, down):
        along(act, me, last, up, down)
        along(act, across, last, up, down)

    def send_line(act, wait, rank):
        other = nearest(z, rank)
        up = jnp.logical_and(other < z, z < DEPTH - 1)
        down = jnp.logical_and(other > z, z > 0)
        if act is drain:
            waits_here = jnp.logical_or(corner, rank < DEPTH - 1)
            up, down = jnp.logical_and(up, waits_here), jnp.logical_and(down, waits_here)
        owner = device(other, y, core)
        for kind in direct:
            wait(owner, kind)
            along(act, owner, kind, up, down)
            over(act, owner, kind)
            beside(act, owner, kind)

    def send_turned(act, wait, rank, up, down):
        other = nearest(z, rank)
        for owner in (device(other, y, core), device(other, 1 - y, core)):
            wait(owner, last)
            along(act, owner, last, up, down)
            beside(act, owner, last)

    def send_crossed(act, wait, rank):
        owner = device(nearest(z, rank), 1 - y, core)
        for kind in direct:
            wait(owner, kind)
            beside(act, owner, kind)

    def wait_long_side():
        owner = device(nearest(z, DEPTH - 1), y, core)
        for kind in direct:
            along(drain, owner, kind, z == 2, z == 1)

    def send_inner_turned(act, wait):
        send_home_turned(act, z == 1, z == 2)
        send_turned(act, wait, 1, z == 1, z == 2)
        if act is start:
            wait_long_side()
        send_home_turned(act, z == 2, z == 1)

        @pl.loop(2, DEPTH)
        def _(rank):
            send_turned(act, wait, rank, z == 2, z == 1)

    def multiply(owner, kind):
        side, start_row, size = pieces[kind]
        own_rows = u_rows if side == 0 else v_rows
        columns = pl.ds(pl.multiple_of(owner * own_rows + start_row, 128), size)
        tokens, total = (grads_here, out_proj) if side == 0 else (acts_here, in_proj)
        total[...] += jnp.dot(tokens[:, columns], piece(owner, kind)[...], preferred_element_type=jnp.float32)

    def multiply_chip(other_z, other_y, kinds):
        @pl.loop(0, CORES)
        def _(turn):
            owner = device(other_z, other_y, jnp.where(turn == 0, core, 1 - core))

            @pl.when(turn == 1)
            def _():
                for kind in kinds:
                    arrived(owner, kind)

            for kind in kinds:
                multiply(owner, kind)

    def multiply_turned(rank):
        other = nearest(z, rank)
        multiply_chip(other, y, (last,))
        multiply_chip(other, 1 - y, (last,))

    loads[0].wait()
    loads[1].wait()
    send_own(start)
    out_proj[...] = jnp.zeros_like(out_proj)
    in_proj[...] = jnp.zeros_like(in_proj)
    loads[2].wait()
    loads[3].wait()
    multiply_chip(z, y, direct)
    arrived(across, last)
    beside(start, across, last)

    def take_crossed(rank):
        send_crossed(start, arrived, rank)
        multiply_chip(nearest(z, rank), 1 - y, direct)

    @pl.loop(1, DEPTH)
    def _(rank):
        send_line(start, arrived, rank)

        @pl.when(jnp.logical_and(corner, rank == 1))
        def _():
            send_home_turned(start, z == 0, z == DEPTH - 1)

        @pl.when(jnp.logical_and(inner, rank == DEPTH - 1))
        def _():
            send_inner_turned(start, arrived)

        behind = jnp.where(corner, rank - 1, rank - 2)

        @pl.when(behind >= 0)
        def _():
            take_crossed(behind)

        multiply_chip(nearest(z, rank), y, direct)

    multiply_turned(0)

    @pl.when(inner)
    def _():
        take_crossed(DEPTH - 2)

    @pl.loop(1, DEPTH - 1)
    def _(rank):
        @pl.when(corner)
        def _():
            send_turned(start, arrived, rank, False, False)

        multiply_turned(rank)

    send_crossed(start, arrived, DEPTH - 1)

    @pl.when(corner)
    def _():
        send_turned(start, arrived, DEPTH - 1, False, False)

    multiply_chip(nearest(z, DEPTH - 1), 1 - y, direct)
    multiply_turned(DEPTH - 1)

    first_slot = me * rows
    live_count = lengths[first_slot // LENGTH]
    offsets = lax.rem(first_slot, LENGTH) + lax.broadcasted_iota(jnp.int32, out_proj.shape, 0)
    product = out_proj[...] * in_proj[...]
    parts[me] = jnp.sum(jnp.where(offsets < live_count, product, 0.0), axis=0, keepdims=True)

    def part_copy(step):
        target = lax.rem(me + step, members)
        return pltpu.make_async_remote_copy(
            src_ref=parts.at[me],
            dst_ref=parts.at[me],
            send_sem=part_send_sem.at[step],
            recv_sem=part_recv_sem.at[step],
            device_id={"query": target},
            device_id_type=MESH,
        )

    @pl.loop(1, members)
    def _(step):
        part_copy(step).start()

    def no_wait(owner, kind):
        pass

    send_own(drain)
    beside(drain, across, last)

    @pl.loop(1, DEPTH)
    def _(rank):
        send_line(drain, no_wait, rank)

    @pl.loop(0, DEPTH)
    def _(rank):
        send_crossed(drain, no_wait, rank)

    @pl.when(corner)
    def _():
        send_home_turned(drain, z == 0, z == DEPTH - 1)

        @pl.loop(1, DEPTH)
        def _(rank):
            send_turned(drain, no_wait, rank, False, False)

    @pl.when(inner)
    def _():
        send_inner_turned(drain, no_wait)

    @pl.loop(1, members)
    def _(step):
        part_copy(step).wait()

    query_count, seq_count = out.shape
    shape = (query_count, parts.shape[2])
    mine = lax.broadcasted_iota(jnp.int32, shape, 1) // RANK == lax.broadcasted_iota(jnp.int32, shape, 0)
    columns = []
    for seq in range(seq_count):
        total = sum(parts[owner] for owner in range(members) if owner * rows // LENGTH == seq)
        columns.append(jnp.sum(jnp.where(mine, total, 0.0), axis=1, keepdims=True))
    out[...] = jnp.concatenate(columns, axis=1)


def fused(acts, grads, u_factor, v_factor, lengths):
    members = lax.axis_size("query")
    rows, factor_cols = acts.shape[0], u_factor.shape[1]
    u_rows, v_rows = u_factor.shape[0], v_factor.shape[0]
    u_cut = -(-u_rows // 256) * 128
    v_cut = v_rows // 256 * 128
    pieces = ((0, 0, u_cut), (0, u_cut, u_rows - u_cut), (1, 0, v_cut), (1, v_cut, v_rows - v_cut))
    hbm = pl.BlockSpec(memory_space=pl.ANY)
    return pl.pallas_call(
        functools.partial(kernel, pieces),
        out_shape=jax.ShapeDtypeStruct((factor_cols // RANK, lengths.shape[0]), jnp.float32),
        in_specs=[pl.BlockSpec(memory_space=pltpu.SMEM), hbm, hbm, hbm, hbm],
        out_specs=pl.BlockSpec(memory_space=pltpu.VMEM),
        scratch_shapes=[
            pltpu.VMEM((members, u_rows, factor_cols), u_factor.dtype),
            pltpu.VMEM((members, v_rows, factor_cols), v_factor.dtype),
            pltpu.VMEM(grads.shape, grads.dtype),
            pltpu.VMEM(acts.shape, acts.dtype),
            pltpu.VMEM((rows, factor_cols), jnp.float32),
            pltpu.VMEM((rows, factor_cols), jnp.float32),
            pltpu.VMEM((members, 1, factor_cols), jnp.float32),
            pltpu.SemaphoreType.DMA((4,)),
            pltpu.SemaphoreType.DMA((4, members, len(pieces))),
            pltpu.SemaphoreType.DMA((members, len(pieces))),
            pltpu.SemaphoreType.DMA((members,)),
            pltpu.SemaphoreType.DMA((members,)),
        ],
        compiler_params=pltpu.CompilerParams(
            collective_id=0, has_side_effects=True, vmem_limit_bytes=56 * 1024 * 1024
        ),
        cost_estimate=pl.CostEstimate(
            flops=2 * rows * factor_cols * members * (u_rows + v_rows),
            bytes_accessed=2 * (acts.size + grads.size + u_factor.size + v_factor.size),
            transcendentals=0,
        ),
    )(lengths, grads, acts, u_factor, v_factor)


def gathered(acts, grads, u_factor, v_factor, lengths):
    rows_here = acts.shape[0]
    members = lax.axis_size("query")
    factor_cols = u_factor.shape[1]
    grads_blocks = grads.reshape(rows_here, members, u_factor.shape[0])
    acts_blocks = acts.reshape(rows_here, members, v_factor.shape[0])
    u_whole = lax.all_gather(u_factor[None], "query", axis=0, tiled=True)
    v_whole = lax.all_gather(v_factor[None], "query", axis=0, tiled=True)
    out_proj = jnp.einsum("tkf,kfc->tc", grads_blocks, u_whole, preferred_element_type=jnp.float32)
    in_proj = jnp.einsum("tkf,kfc->tc", acts_blocks, v_whole, preferred_element_type=jnp.float32)
    token_score = (out_proj * in_proj).reshape(rows_here, factor_cols // RANK, RANK).sum(axis=2)
    first_slot = lax.axis_index("query") * rows_here
    offsets = first_slot % LENGTH + jnp.arange(rows_here, dtype=jnp.int32)
    selector = jnp.arange(lengths.shape[0], dtype=jnp.int32) == first_slot // LENGTH
    live_count = jnp.sum(jnp.where(selector, lengths, jnp.zeros_like(lengths)))
    live = (offsets < live_count).astype(jnp.float32)
    query_sums = jnp.sum(token_score * live[:, None], axis=0)
    return lax.psum(query_sums[:, None] * selector.astype(jnp.float32)[None, :], "query")


def solution(mesh):
    whole_grid = mesh.shape["query"] == DEPTH * WIDTH * CORES
    return jax.shard_map(
        fused if whole_grid else gathered,
        mesh=mesh,
        in_specs=(
            P(("grp", "query"), None),
            P(("grp", "query"), None),
            P(("grp", "query"), None),
            P(("grp", "query"), None),
            P("grp"),
        ),
        out_specs=P("grp", None),
        check_vma=False,
    )
```

```python
import functools

import jax
import jax.numpy as jnp
from jax import lax
from jax.experimental import pallas as pl
from jax.experimental.pallas import tpu as pltpu
from jax.sharding import PartitionSpec as P

RANK = 32
LENGTH = 2048
MESH = pl.DeviceIdType.MESH
DEPTH, WIDTH, CORES = 4, 2, 2
UP, DOWN, ACROSS, SIBLING = range(4)
LENT_CHUNKS = 2


def device(z, y, core):
    return (z * WIDTH + y) * CORES + core


def nearest(z, rank):
    near = jnp.where(z < 2, z, 3 - z)
    swapped = jnp.where(rank == 0, 1, jnp.where(rank == 1, 0, rank))
    found = jnp.where(near == 0, rank, swapped)
    return jnp.where(z < 2, found, 3 - found)


def kernel(pieces, lengths, grads, acts, u_own, v_own, out, u_all, v_all, grads_here, acts_here, out_proj, in_proj,
           acts_lent, part_lent, part_back, parts, load_sem, send_sem, recv_sem, lend_sem, back_sem,
           part_send_sem, part_recv_sem):
    me = lax.axis_index("query")
    members = u_all.shape[0]
    core = lax.rem(me, CORES)
    y = lax.rem(me // CORES, WIDTH)
    z = me // (CORES * WIDTH)
    sibling = device(z, y, 1 - core)
    across = device(z, 1 - y, core)
    u_rows, v_rows = u_own.shape[0], v_own.shape[0]
    rows = grads.shape[0]

    loads = [
        pltpu.make_async_copy(u_own, u_all.at[me], load_sem.at[0]),
        pltpu.make_async_copy(v_own, v_all.at[me], load_sem.at[1]),
        pltpu.make_async_copy(grads, grads_here, load_sem.at[2]),
        pltpu.make_async_copy(acts, acts_here, load_sem.at[3]),
    ]
    for load in loads:
        load.start()

    barrier = pltpu.get_barrier_semaphore()

    @pl.loop(1, members)
    def _(step):
        pl.semaphore_signal(barrier, inc=1, device_id={"query": lax.rem(me + step, members)}, device_id_type=MESH)

    pl.semaphore_wait(barrier, members - 1)

    def piece(owner, kind):
        side, start, size = pieces[kind]
        return (u_all if side == 0 else v_all).at[owner, pl.ds(start, size)]

    def copy(owner, kind, way, target):
        return pltpu.make_async_remote_copy(
            src_ref=piece(owner, kind),
            dst_ref=piece(owner, kind),
            send_sem=send_sem.at[way, owner, kind],
            recv_sem=recv_sem.at[owner, kind],
            device_id={"query": target},
            device_id_type=MESH,
        )

    def start(one):
        one.start()

    def drain(one):
        one.wait_send()

    def arrived(owner, kind):
        copy(owner, kind, SIBLING, sibling).wait_recv()

    direct, turned = (0, 1), (2, 3)

    def along(act, owner, kind, up, down):
        @pl.when(up)
        def _():
            act(copy(owner, kind, UP, device(z + 1, y, core)))

        @pl.when(down)
        def _():
            act(copy(owner, kind, DOWN, device(z - 1, y, core)))

    def over(act, owner, kind):
        act(copy(owner, kind, ACROSS, across))

    def beside(act, owner, kind):
        act(copy(owner, kind, SIBLING, sibling))

    corner = jnp.logical_or(z == 0, z == DEPTH - 1)
    inner = jnp.logical_not(corner)

    def send_own(act):
        for kind in turned:
            over(act, me, kind)
        for kind in direct:
            along(act, me, kind, z < DEPTH - 1, z > 0)
            over(act, me, kind)
        for kind in direct + turned:
            beside(act, me, kind)

    def wait_own_along():
        for kind in direct:
            along(drain, me, kind, z == 0, z == DEPTH - 1)

    def send_home_turned(act):
        for owner in (me, across):
            for kind in turned:
                along(act, owner, kind, z < 2, z >= 2)

    def send_line(act, wait, rank):
        other = nearest(z, rank)
        up = jnp.logical_and(other < z, z < DEPTH - 1)
        down = jnp.logical_and(other > z, z > 0)
        owner = device(other, y, core)
        for kind in direct:
            wait(owner, kind)
            along(act, owner, kind, up, down)
            over(act, owner, kind)
            beside(act, owner, kind)

    def send_turned(act, wait, rank, up, down):
        other = nearest(z, rank)
        for owner in (device(other, y, core), device(other, 1 - y, core)):
            for kind in turned:
                wait(owner, kind)
                along(act, owner, kind, up, down)
                beside(act, owner, kind)

    def send_crossed(act, wait, rank):
        owner = device(nearest(z, rank), 1 - y, core)
        for kind in direct:
            wait(owner, kind)
            beside(act, owner, kind)

    inward = device(jnp.where(z < 2, z + 1, z - 1), y, core)
    outward = device(jnp.where(z < 2, z - 1, z + 1), y, core)
    first_lent = CORES * WIDTH
    lent = members - 2 * first_lent
    lent_rows = rows // LENT_CHUNKS

    def lend(chunk):
        here = pl.ds(chunk * lent_rows, lent_rows)
        return pltpu.make_async_remote_copy(
            src_ref=acts_here.at[here, pl.ds(first_lent * v_rows, lent * v_rows)],
            dst_ref=acts_lent.at[here],
            send_sem=lend_sem.at[0, chunk],
            recv_sem=lend_sem.at[1, chunk],
            device_id={"query": inward},
            device_id_type=MESH,
        )

    def give_back(chunk):
        here = pl.ds(chunk * lent_rows, lent_rows)
        return pltpu.make_async_remote_copy(
            src_ref=part_lent.at[here],
            dst_ref=part_back.at[here],
            send_sem=back_sem.at[0, chunk],
            recv_sem=back_sem.at[1, chunk],
            device_id={"query": outward},
            device_id_type=MESH,
        )

    def work_lent(chunk):
        here = pl.ds(chunk * lent_rows, lent_rows)
        lend(chunk).wait_recv()
        part_lent[here] = jnp.zeros((lent_rows, part_lent.shape[1]), jnp.float32)

        @pl.loop(0, lent)
        def _(turn):
            columns = pl.ds(pl.multiple_of(turn * v_rows, 128), v_rows)
            part_lent[here] += jnp.dot(
                acts_lent[here, columns], v_all[first_lent + turn], preferred_element_type=jnp.float32
            )

        give_back(chunk).start()

    def multiply(owner, kind):
        side, start_row, size = pieces[kind]
        own_rows = u_rows if side == 0 else v_rows
        columns = pl.ds(pl.multiple_of(owner * own_rows + start_row, 128), size)
        tokens, total = (grads_here, out_proj) if side == 0 else (acts_here, in_proj)
        total[...] += jnp.dot(tokens[:, columns], piece(owner, kind)[...], preferred_element_type=jnp.float32)

    def multiply_chip(other_z, other_y, kinds):
        @pl.loop(0, CORES)
        def _(turn):
            owner = device(other_z, other_y, jnp.where(turn == 0, core, 1 - core))

            @pl.when(turn == 1)
            def _():
                for kind in kinds:
                    arrived(owner, kind)

            for kind in kinds:
                multiply(owner, kind)

    def multiply_turned(rank):
        other = nearest(z, rank)
        multiply_chip(other, y, turned)
        multiply_chip(other, 1 - y, turned)

    loads[0].wait()
    loads[1].wait()
    send_own(start)
    out_proj[...] = jnp.zeros_like(out_proj)
    in_proj[...] = jnp.zeros_like(in_proj)
    loads[2].wait()
    loads[3].wait()
    multiply_chip(z, y, direct)
    for kind in turned:
        arrived(across, kind)
        beside(start, across, kind)

    def take_crossed(rank):
        send_crossed(start, arrived, rank)
        multiply_chip(nearest(z, rank), 1 - y, direct)

    @pl.loop(1, DEPTH)
    def _(rank):
        send_line(start, arrived, rank)

        @pl.when(jnp.logical_and(corner, rank == 1))
        def _():
            wait_own_along()
            send_home_turned(start)

        @pl.when(jnp.logical_and(corner, rank == 2))
        def _():
            send_home_turned(drain)
            lend(0).start()

        @pl.when(jnp.logical_and(corner, rank == 3))
        def _():
            for chunk in range(1, LENT_CHUNKS):
                lend(chunk - 1).wait_send()
                lend(chunk).start()

        @pl.when(jnp.logical_and(inner, rank == 3))
        def _():
            send_home_turned(start)

        behind = jnp.where(corner, rank - 1, rank - 3)

        @pl.when(behind >= 0)
        def _():
            take_crossed(behind)

        multiply_chip(nearest(z, rank), y, direct)

    multiply_turned(0)

    @pl.when(inner)
    def _():
        send_home_turned(drain)
        send_turned(start, arrived, 1, z == 1, z == 2)
        send_turned(start, arrived, 2, False, False)
        multiply_turned(2)
        for chunk in range(LENT_CHUNKS - 1):
            work_lent(chunk)
        send_turned(start, arrived, 3, z == 2, z == 1)
        work_lent(LENT_CHUNKS - 1)
        take_crossed(1)
        take_crossed(2)
        multiply_turned(1)

    send_crossed(start, arrived, DEPTH - 1)

    @pl.when(corner)
    def _():
        send_turned(start, arrived, DEPTH - 1, False, False)

    multiply_chip(nearest(z, DEPTH - 1), 1 - y, direct)
    multiply_turned(DEPTH - 1)

    @pl.when(corner)
    def _():
        for chunk in range(LENT_CHUNKS):
            give_back(chunk).wait_recv()
        in_proj[...] += part_back[...]

    first_slot = me * rows
    live_count = lengths[first_slot // LENGTH]
    offsets = lax.rem(first_slot, LENGTH) + lax.broadcasted_iota(jnp.int32, out_proj.shape, 0)
    product = out_proj[...] * in_proj[...]
    parts[me] = jnp.sum(jnp.where(offsets < live_count, product, 0.0), axis=0, keepdims=True)

    def part_copy(step):
        target = lax.rem(me + step, members)
        return pltpu.make_async_remote_copy(
            src_ref=parts.at[me],
            dst_ref=parts.at[me],
            send_sem=part_send_sem.at[step],
            recv_sem=part_recv_sem.at[step],
            device_id={"query": target},
            device_id_type=MESH,
        )

    @pl.loop(1, members)
    def _(step):
        part_copy(step).start()

    def no_wait(owner, kind):
        pass

    for kind in turned:
        over(drain, me, kind)
    for kind in direct:
        along(drain, me, kind, inner, inner)
        over(drain, me, kind)
    for kind in direct + turned:
        beside(drain, me, kind)
    for kind in turned:
        beside(drain, across, kind)

    @pl.loop(1, DEPTH)
    def _(rank):
        send_line(drain, no_wait, rank)

    @pl.loop(0, DEPTH)
    def _(rank):
        send_crossed(drain, no_wait, rank)

    @pl.when(corner)
    def _():
        send_turned(drain, no_wait, DEPTH - 1, False, False)
        lend(LENT_CHUNKS - 1).wait_send()

    @pl.when(inner)
    def _():
        send_turned(drain, no_wait, 1, z == 1, z == 2)
        send_turned(drain, no_wait, 2, False, False)
        send_turned(drain, no_wait, 3, z == 2, z == 1)
        for chunk in range(LENT_CHUNKS):
            give_back(chunk).wait_send()

    @pl.loop(1, members)
    def _(step):
        part_copy(step).wait()

    query_count, seq_count = out.shape
    shape = (query_count, parts.shape[2])
    mine = lax.broadcasted_iota(jnp.int32, shape, 1) // RANK == lax.broadcasted_iota(jnp.int32, shape, 0)
    columns = []
    for seq in range(seq_count):
        total = sum(parts[owner] for owner in range(members) if owner * rows // LENGTH == seq)
        columns.append(jnp.sum(jnp.where(mine, total, 0.0), axis=1, keepdims=True))
    out[...] = jnp.concatenate(columns, axis=1)


def fused(acts, grads, u_factor, v_factor, lengths):
    members = lax.axis_size("query")
    rows, factor_cols = acts.shape[0], u_factor.shape[1]
    u_rows, v_rows = u_factor.shape[0], v_factor.shape[0]
    u_cut = -(-u_rows // 256) * 128
    v_cut = v_rows // 256 * 128
    pieces = ((0, 0, u_cut), (0, u_cut, u_rows - u_cut), (1, 0, v_cut), (1, v_cut, v_rows - v_cut))
    hbm = pl.BlockSpec(memory_space=pl.ANY)
    return pl.pallas_call(
        functools.partial(kernel, pieces),
        out_shape=jax.ShapeDtypeStruct((factor_cols // RANK, lengths.shape[0]), jnp.float32),
        in_specs=[pl.BlockSpec(memory_space=pltpu.SMEM), hbm, hbm, hbm, hbm],
        out_specs=pl.BlockSpec(memory_space=pltpu.VMEM),
        scratch_shapes=[
            pltpu.VMEM((members, u_rows, factor_cols), u_factor.dtype),
            pltpu.VMEM((members, v_rows, factor_cols), v_factor.dtype),
            pltpu.VMEM(grads.shape, grads.dtype),
            pltpu.VMEM(acts.shape, acts.dtype),
            pltpu.VMEM((rows, factor_cols), jnp.float32),
            pltpu.VMEM((rows, factor_cols), jnp.float32),
            pltpu.VMEM((rows, (members - 2 * CORES * WIDTH) * v_rows), acts.dtype),
            pltpu.VMEM((rows, factor_cols), jnp.float32),
            pltpu.VMEM((rows, factor_cols), jnp.float32),
            pltpu.VMEM((members, 1, factor_cols), jnp.float32),
            pltpu.SemaphoreType.DMA((4,)),
            pltpu.SemaphoreType.DMA((4, members, len(pieces))),
            pltpu.SemaphoreType.DMA((members, len(pieces))),
            pltpu.SemaphoreType.DMA((2, LENT_CHUNKS)),
            pltpu.SemaphoreType.DMA((2, LENT_CHUNKS)),
            pltpu.SemaphoreType.DMA((members,)),
            pltpu.SemaphoreType.DMA((members,)),
        ],
        compiler_params=pltpu.CompilerParams(
            collective_id=0, has_side_effects=True, vmem_limit_bytes=56 * 1024 * 1024
        ),
        cost_estimate=pl.CostEstimate(
            flops=2 * rows * factor_cols * members * (u_rows + v_rows),
            bytes_accessed=2 * (acts.size + grads.size + u_factor.size + v_factor.size),
            transcendentals=0,
        ),
    )(lengths, grads, acts, u_factor, v_factor)


def gathered(acts, grads, u_factor, v_factor, lengths):
    rows_here = acts.shape[0]
    members = lax.axis_size("query")
    factor_cols = u_factor.shape[1]
    grads_blocks = grads.reshape(rows_here, members, u_factor.shape[0])
    acts_blocks = acts.reshape(rows_here, members, v_factor.shape[0])
    u_whole = lax.all_gather(u_factor[None], "query", axis=0, tiled=True)
    v_whole = lax.all_gather(v_factor[None], "query", axis=0, tiled=True)
    out_proj = jnp.einsum("tkf,kfc->tc", grads_blocks, u_whole, preferred_element_type=jnp.float32)
    in_proj = jnp.einsum("tkf,kfc->tc", acts_blocks, v_whole, preferred_element_type=jnp.float32)
    token_score = (out_proj * in_proj).reshape(rows_here, factor_cols // RANK, RANK).sum(axis=2)
    first_slot = lax.axis_index("query") * rows_here
    offsets = first_slot % LENGTH + jnp.arange(rows_here, dtype=jnp.int32)
    selector = jnp.arange(lengths.shape[0], dtype=jnp.int32) == first_slot // LENGTH
    live_count = jnp.sum(jnp.where(selector, lengths, jnp.zeros_like(lengths)))
    live = (offsets < live_count).astype(jnp.float32)
    query_sums = jnp.sum(token_score * live[:, None], axis=0)
    return lax.psum(query_sums[:, None] * selector.astype(jnp.float32)[None, :], "query")


def solution(mesh):
    whole_grid = mesh.shape["query"] == DEPTH * WIDTH * CORES
    return jax.shard_map(
        fused if whole_grid else gathered,
        mesh=mesh,
        in_specs=(
            P(("grp", "query"), None),
            P(("grp", "query"), None),
            P(("grp", "query"), None),
            P(("grp", "query"), None),
            P("grp"),
        ),
        out_specs=P("grp", None),
        check_vma=False,
    )
```

```python
import functools

import jax
import jax.numpy as jnp
from jax import lax
from jax.experimental import pallas as pl
from jax.experimental.pallas import tpu as pltpu
from jax.sharding import PartitionSpec as P

RANK = 32
LENGTH = 2048
MESH = pl.DeviceIdType.MESH
DEPTH, WIDTH, CORES = 4, 2, 2
UP, DOWN, ACROSS, SIBLING = range(4)
LENT_CHUNKS = 2


def device(z, y, core):
    return (z * WIDTH + y) * CORES + core


def nearest(z, rank):
    near = jnp.where(z < 2, z, 3 - z)
    swapped = jnp.where(rank == 0, 1, jnp.where(rank == 1, 0, rank))
    found = jnp.where(near == 0, rank, swapped)
    return jnp.where(z < 2, found, 3 - found)


def kernel(pieces, lengths, grads, acts, u_own, v_own, out, u_all, v_all, grads_here, acts_here, out_proj, in_proj,
           acts_lent, part_lent, part_back, parts, load_sem, send_sem, recv_sem, lend_sem, back_sem,
           part_send_sem, part_recv_sem):
    me = lax.axis_index("query")
    members = u_all.shape[0]
    core = lax.rem(me, CORES)
    y = lax.rem(me // CORES, WIDTH)
    z = me // (CORES * WIDTH)
    sibling = device(z, y, 1 - core)
    across = device(z, 1 - y, core)
    u_rows, v_rows = u_own.shape[0], v_own.shape[0]
    rows = grads.shape[0]

    loads = [
        pltpu.make_async_copy(u_own, u_all.at[me], load_sem.at[0]),
        pltpu.make_async_copy(v_own, v_all.at[me], load_sem.at[1]),
        pltpu.make_async_copy(grads, grads_here, load_sem.at[2]),
        pltpu.make_async_copy(acts, acts_here, load_sem.at[3]),
    ]
    for load in loads:
        load.start()

    barrier = pltpu.get_barrier_semaphore()

    @pl.loop(1, members)
    def _(step):
        pl.semaphore_signal(barrier, inc=1, device_id={"query": lax.rem(me + step, members)}, device_id_type=MESH)

    pl.semaphore_wait(barrier, members - 1)

    def piece(owner, kind):
        side, start, size = pieces[kind]
        return (u_all if side == 0 else v_all).at[owner, pl.ds(start, size)]

    def copy(owner, kind, way, target):
        return pltpu.make_async_remote_copy(
            src_ref=piece(owner, kind),
            dst_ref=piece(owner, kind),
            send_sem=send_sem.at[way, owner, kind],
            recv_sem=recv_sem.at[owner, kind],
            device_id={"query": target},
            device_id_type=MESH,
        )

    def start(one):
        one.start()

    def drain(one):
        one.wait_send()

    def arrived(owner, kind):
        copy(owner, kind, SIBLING, sibling).wait_recv()

    direct, turned = (0,), (1,)

    def along(act, owner, kind, up, down):
        @pl.when(up)
        def _():
            act(copy(owner, kind, UP, device(z + 1, y, core)))

        @pl.when(down)
        def _():
            act(copy(owner, kind, DOWN, device(z - 1, y, core)))

    def over(act, owner, kind):
        act(copy(owner, kind, ACROSS, across))

    def beside(act, owner, kind):
        act(copy(owner, kind, SIBLING, sibling))

    corner = jnp.logical_or(z == 0, z == DEPTH - 1)
    inner = jnp.logical_not(corner)

    def send_own(act):
        for kind in turned:
            over(act, me, kind)
        for kind in direct:
            along(act, me, kind, z < DEPTH - 1, z > 0)
            over(act, me, kind)
        for kind in direct + turned:
            beside(act, me, kind)

    def wait_own_along():
        for kind in direct:
            along(drain, me, kind, z == 0, z == DEPTH - 1)

    def send_home_turned(act):
        for owner in (me, across):
            for kind in turned:
                along(act, owner, kind, z < 2, z >= 2)

    def send_line(act, wait, rank):
        other = nearest(z, rank)
        up = jnp.logical_and(other < z, z < DEPTH - 1)
        down = jnp.logical_and(other > z, z > 0)
        owner = device(other, y, core)
        for kind in direct:
            wait(owner, kind)
            along(act, owner, kind, up, down)
            over(act, owner, kind)
            beside(act, owner, kind)

    def send_turned(act, wait, rank, up, down):
        other = nearest(z, rank)
        for owner in (device(other, y, core), device(other, 1 - y, core)):
            for kind in turned:
                wait(owner, kind)
                along(act, owner, kind, up, down)
                beside(act, owner, kind)

    def send_crossed(act, wait, rank):
        owner = device(nearest(z, rank), 1 - y, core)
        for kind in direct:
            wait(owner, kind)
            beside(act, owner, kind)

    def wait_corner_turned():
        other = nearest(z, 1)
        for owner in (device(other, y, core), device(other, 1 - y, core)):
            for kind in turned:
                along(drain, owner, kind, z == 1, z == 2)

    inward = device(jnp.where(z < 2, z + 1, z - 1), y, core)
    outward = device(jnp.where(z < 2, z - 1, z + 1), y, core)
    first_lent = CORES * WIDTH
    lent = members - 2 * first_lent
    lent_rows = rows // LENT_CHUNKS

    def lend(chunk):
        here = pl.ds(chunk * lent_rows, lent_rows)
        return pltpu.make_async_remote_copy(
            src_ref=acts_here.at[here, pl.ds(first_lent * v_rows, lent * v_rows)],
            dst_ref=acts_lent.at[here],
            send_sem=lend_sem.at[0, chunk],
            recv_sem=lend_sem.at[1, chunk],
            device_id={"query": inward},
            device_id_type=MESH,
        )

    def give_back(chunk):
        here = pl.ds(chunk * lent_rows, lent_rows)
        return pltpu.make_async_remote_copy(
            src_ref=part_lent.at[here],
            dst_ref=part_back.at[here],
            send_sem=back_sem.at[0, chunk],
            recv_sem=back_sem.at[1, chunk],
            device_id={"query": outward},
            device_id_type=MESH,
        )

    def work_lent(chunk):
        here = pl.ds(chunk * lent_rows, lent_rows)
        lend(chunk).wait_recv()
        part_lent[here] = jnp.zeros((lent_rows, part_lent.shape[1]), jnp.float32)

        @pl.loop(0, lent)
        def _(turn):
            columns = pl.ds(pl.multiple_of(turn * v_rows, 128), v_rows)
            part_lent[here] += jnp.dot(
                acts_lent[here, columns], v_all[first_lent + turn], preferred_element_type=jnp.float32
            )

        give_back(chunk).start()

    def multiply(owner, kind):
        side, start_row, size = pieces[kind]
        own_rows = u_rows if side == 0 else v_rows
        columns = pl.ds(pl.multiple_of(owner * own_rows + start_row, 128), size)
        tokens, total = (grads_here, out_proj) if side == 0 else (acts_here, in_proj)
        total[...] += jnp.dot(tokens[:, columns], piece(owner, kind)[...], preferred_element_type=jnp.float32)

    def multiply_chip(other_z, other_y, kinds):
        @pl.loop(0, CORES)
        def _(turn):
            owner = device(other_z, other_y, jnp.where(turn == 0, core, 1 - core))

            @pl.when(turn == 1)
            def _():
                for kind in kinds:
                    arrived(owner, kind)

            for kind in kinds:
                multiply(owner, kind)

    def multiply_turned(rank):
        other = nearest(z, rank)
        multiply_chip(other, y, turned)
        multiply_chip(other, 1 - y, turned)

    loads[0].wait()
    loads[1].wait()
    send_own(start)
    out_proj[...] = jnp.zeros_like(out_proj)
    in_proj[...] = jnp.zeros_like(in_proj)
    loads[2].wait()
    loads[3].wait()
    multiply_chip(z, y, direct)

    def take_neighbours_turned():
        for kind in turned:
            arrived(across, kind)
            beside(start, across, kind)

    def take_crossed(rank):
        send_crossed(start, arrived, rank)
        multiply_chip(nearest(z, rank), 1 - y, direct)

    @pl.loop(1, DEPTH)
    def _(rank):
        send_line(start, arrived, rank)

        @pl.when(jnp.logical_and(corner, rank == 1))
        def _():
            wait_own_along()
            take_neighbours_turned()
            send_home_turned(start)

        @pl.when(jnp.logical_and(corner, rank == 2))
        def _():
            send_home_turned(drain)
            lend(0).start()

        @pl.when(jnp.logical_and(corner, rank == 3))
        def _():
            for chunk in range(1, LENT_CHUNKS):
                lend(chunk - 1).wait_send()
                lend(chunk).start()

        @pl.when(jnp.logical_and(inner, rank == 3))
        def _():
            take_neighbours_turned()
            send_turned(start, arrived, 1, z == 1, z == 2)

        behind = jnp.where(corner, rank - 1, rank - 3)

        @pl.when(behind >= 0)
        def _():
            take_crossed(behind)

        multiply_chip(nearest(z, rank), y, direct)

    multiply_turned(0)

    @pl.when(inner)
    def _():
        wait_corner_turned()
        send_home_turned(start)
        send_turned(start, arrived, 3, z == 2, z == 1)
        send_turned(start, arrived, 2, False, False)
        multiply_turned(2)
        for chunk in range(LENT_CHUNKS):
            work_lent(chunk)
        take_crossed(1)
        take_crossed(2)
        multiply_turned(1)

    def no_wait(owner, kind):
        pass

    for kind in turned:
        over(drain, me, kind)
    for kind in direct:
        along(drain, me, kind, inner, inner)
        over(drain, me, kind)
    for kind in direct + turned:
        beside(drain, me, kind)
    for kind in turned:
        beside(drain, across, kind)

    send_line(drain, no_wait, 1)
    send_crossed(drain, no_wait, 0)
    send_crossed(drain, no_wait, 1)

    send_crossed(start, arrived, DEPTH - 1)

    @pl.when(corner)
    def _():
        send_turned(start, arrived, DEPTH - 1, False, False)

    multiply_chip(nearest(z, DEPTH - 1), 1 - y, direct)
    multiply_turned(DEPTH - 1)

    @pl.when(corner)
    def _():
        for chunk in range(LENT_CHUNKS):
            give_back(chunk).wait_recv()
        in_proj[...] += part_back[...]

    first_slot = me * rows
    live_count = lengths[first_slot // LENGTH]
    offsets = lax.rem(first_slot, LENGTH) + lax.broadcasted_iota(jnp.int32, out_proj.shape, 0)
    product = out_proj[...] * in_proj[...]
    parts[me] = jnp.sum(jnp.where(offsets < live_count, product, 0.0), axis=0, keepdims=True)

    def part_copy(step):
        target = lax.rem(me + step, members)
        return pltpu.make_async_remote_copy(
            src_ref=parts.at[me],
            dst_ref=parts.at[me],
            send_sem=part_send_sem.at[step],
            recv_sem=part_recv_sem.at[step],
            device_id={"query": target},
            device_id_type=MESH,
        )

    @pl.loop(1, members)
    def _(step):
        part_copy(step).start()

    @pl.loop(2, DEPTH)
    def _(rank):
        send_line(drain, no_wait, rank)

    @pl.loop(2, DEPTH)
    def _(rank):
        send_crossed(drain, no_wait, rank)

    @pl.when(corner)
    def _():
        send_turned(drain, no_wait, DEPTH - 1, False, False)
        lend(LENT_CHUNKS - 1).wait_send()

    @pl.when(inner)
    def _():
        send_home_turned(drain)
        send_turned(drain, no_wait, 1, False, False)
        send_turned(drain, no_wait, 2, False, False)
        send_turned(drain, no_wait, 3, z == 2, z == 1)
        for chunk in range(LENT_CHUNKS):
            give_back(chunk).wait_send()

    @pl.loop(1, members)
    def _(step):
        part_copy(step).wait()

    query_count, seq_count = out.shape
    shape = (query_count, parts.shape[2])
    mine = lax.broadcasted_iota(jnp.int32, shape, 1) // RANK == lax.broadcasted_iota(jnp.int32, shape, 0)
    columns = []
    for seq in range(seq_count):
        total = sum(parts[owner] for owner in range(members) if owner * rows // LENGTH == seq)
        columns.append(jnp.sum(jnp.where(mine, total, 0.0), axis=1, keepdims=True))
    out[...] = jnp.concatenate(columns, axis=1)


def fused(acts, grads, u_factor, v_factor, lengths):
    members = lax.axis_size("query")
    rows, factor_cols = acts.shape[0], u_factor.shape[1]
    u_rows, v_rows = u_factor.shape[0], v_factor.shape[0]
    pieces = ((0, 0, u_rows), (1, 0, v_rows))
    hbm = pl.BlockSpec(memory_space=pl.ANY)
    return pl.pallas_call(
        functools.partial(kernel, pieces),
        out_shape=jax.ShapeDtypeStruct((factor_cols // RANK, lengths.shape[0]), jnp.float32),
        in_specs=[pl.BlockSpec(memory_space=pltpu.SMEM), hbm, hbm, hbm, hbm],
        out_specs=pl.BlockSpec(memory_space=pltpu.VMEM),
        scratch_shapes=[
            pltpu.VMEM((members, u_rows, factor_cols), u_factor.dtype),
            pltpu.VMEM((members, v_rows, factor_cols), v_factor.dtype),
            pltpu.VMEM(grads.shape, grads.dtype),
            pltpu.VMEM(acts.shape, acts.dtype),
            pltpu.VMEM((rows, factor_cols), jnp.float32),
            pltpu.VMEM((rows, factor_cols), jnp.float32),
            pltpu.VMEM((rows, (members - 2 * CORES * WIDTH) * v_rows), acts.dtype),
            pltpu.VMEM((rows, factor_cols), jnp.float32),
            pltpu.VMEM((rows, factor_cols), jnp.float32),
            pltpu.VMEM((members, 1, factor_cols), jnp.float32),
            pltpu.SemaphoreType.DMA((4,)),
            pltpu.SemaphoreType.DMA((4, members, len(pieces))),
            pltpu.SemaphoreType.DMA((members, len(pieces))),
            pltpu.SemaphoreType.DMA((2, LENT_CHUNKS)),
            pltpu.SemaphoreType.DMA((2, LENT_CHUNKS)),
            pltpu.SemaphoreType.DMA((members,)),
            pltpu.SemaphoreType.DMA((members,)),
        ],
        compiler_params=pltpu.CompilerParams(
            collective_id=0, has_side_effects=True, vmem_limit_bytes=56 * 1024 * 1024
        ),
        cost_estimate=pl.CostEstimate(
            flops=2 * rows * factor_cols * members * (u_rows + v_rows),
            bytes_accessed=2 * (acts.size + grads.size + u_factor.size + v_factor.size),
            transcendentals=0,
        ),
    )(lengths, grads, acts, u_factor, v_factor)


def gathered(acts, grads, u_factor, v_factor, lengths):
    rows_here = acts.shape[0]
    members = lax.axis_size("query")
    factor_cols = u_factor.shape[1]
    grads_blocks = grads.reshape(rows_here, members, u_factor.shape[0])
    acts_blocks = acts.reshape(rows_here, members, v_factor.shape[0])
    u_whole = lax.all_gather(u_factor[None], "query", axis=0, tiled=True)
    v_whole = lax.all_gather(v_factor[None], "query", axis=0, tiled=True)
    out_proj = jnp.einsum("tkf,kfc->tc", grads_blocks, u_whole, preferred_element_type=jnp.float32)
    in_proj = jnp.einsum("tkf,kfc->tc", acts_blocks, v_whole, preferred_element_type=jnp.float32)
    token_score = (out_proj * in_proj).reshape(rows_here, factor_cols // RANK, RANK).sum(axis=2)
    first_slot = lax.axis_index("query") * rows_here
    offsets = first_slot % LENGTH + jnp.arange(rows_here, dtype=jnp.int32)
    selector = jnp.arange(lengths.shape[0], dtype=jnp.int32) == first_slot // LENGTH
    live_count = jnp.sum(jnp.where(selector, lengths, jnp.zeros_like(lengths)))
    live = (offsets < live_count).astype(jnp.float32)
    query_sums = jnp.sum(token_score * live[:, None], axis=0)
    return lax.psum(query_sums[:, None] * selector.astype(jnp.float32)[None, :], "query")


def solution(mesh):
    whole_grid = mesh.shape["query"] == DEPTH * WIDTH * CORES
    return jax.shard_map(
        fused if whole_grid else gathered,
        mesh=mesh,
        in_specs=(
            P(("grp", "query"), None),
            P(("grp", "query"), None),
            P(("grp", "query"), None),
            P(("grp", "query"), None),
            P("grp"),
        ),
        out_specs=P("grp", None),
        check_vma=False,
    )
```
